512 devices in a mesh: subj: 32 (over z, core), var: 16 (over x, y).
Axes of the slice: x: 4, y: 4, z: 16, core: 2. Of those that a mesh axis runs over, the one named last changes fastest.
Arguments:
- traits: bfloat16 [65536, 256], P('subj', 'var'), may hold values from -6 to 6
- kin_tiles: bfloat16 [384, 256, 256], P('subj'), may hold values from -0.25 to 0.25
- kin_index: int32 [384, 2], P('subj'), may hold values from 0 to 255, as said below
- dosages: bfloat16 [65536, 12288], P('subj', 'var'), may hold values from 0 to 255, as said below
Outputs:
- scores: float32 [12288, 256], P(('var', 'subj'))
The draws below stay inside these ranges and needn't reach their ends.
Inputs may be any that keep to these rules, and one draw needn't show every extreme that they name: `kin_index`: rows t * 12 to (t + 1) * 12 - 1 hold tiles whose row block lies in t * 8 to (t + 1) * 8 - 1; every row block has its diagonal tile; counts per row block are uneven; a pair may repeat. `dosages`: whole numbers.
All inputs are finite; a program needn't handle non-finite values.
Results may differ from the reference program's by a relative error of at most 0.009.
Values may be sent and summed in bfloat16 or wider, within the bound.
No kernel may reach another device: no remote copies, remote signals or barrier semaphores. Data moves between devices by JAX's collectives and lax.ppermute only.
A program may use at most 64 MiB of HBM per device.

```python
import jax
import jax.numpy as jnp
from jax import lax

K = 256
BLOCK = 256
SUBJ_DEV = 2048
VAR_DEV = 768
TILES_DEV = 12
NSUB = 65536
NVAR = 12288
NBLOCKS = 256
NTILES = 384
N_SUBJ = 32
N_VAR = 16


def draw_kin_index(key, part):
    per_dev = SUBJ_DEV // BLOCK
    extra = TILES_DEV - per_dev
    devices = jnp.arange(N_SUBJ, dtype=jnp.int32)
    diag = devices[:, None] * per_dev + jnp.arange(per_dev, dtype=jnp.int32)[None, :]
    key_rows, key_cols = jax.random.split(jax.random.fold_in(key, 11))
    extra_rows = devices[:, None] * per_dev + jax.random.randint(key_rows, (N_SUBJ, extra), 0, per_dev, dtype=jnp.int32)
    extra_cols = jax.random.randint(key_cols, (N_SUBJ, extra), 0, NBLOCKS, dtype=jnp.int32)
    rows_all = jnp.concatenate([diag, extra_rows], axis=1).reshape(-1)
    cols_all = jnp.concatenate([diag, extra_cols], axis=1).reshape(-1)
    return jnp.stack([rows_all, cols_all], axis=1).astype(jnp.int32)


def draw_dosages(key, part):
    codes = jax.random.randint(jax.random.fold_in(key, 23), (NSUB, NVAR), 0, 256, dtype=jnp.int32)
    return codes.astype(jnp.float32).astype(jnp.bfloat16)


def shard_levels(rng, shape, pieces, low, high):
    def one(dim, shards_of):
        heights = jax.random.uniform(jax.random.fold_in(jax.random.fold_in(rng, 6), dim), (shards_of,), jnp.float32, low / len(pieces), high / len(pieces))
        return jnp.repeat(jnp.exp(heights), shape[dim] // shards_of).reshape((-1,) + (1,) * (len(shape) - dim - 1))

    level = one(*pieces[0])
    for cut in pieces[1:]:
        level = level * one(*cut)
    return level


def gaussian(key, shape, spread, reach, pieces=(), kind=jnp.bfloat16):
    factor_of = shard_levels(key, shape, pieces, -0.22, 0.18) if pieces else 1.0
    drawn = jax.random.normal(key, shape, jnp.float32) * spread * factor_of
    return jnp.minimum(jnp.maximum(drawn, -reach), reach).astype(kind)


def setup_inputs(seed: int = 0) -> dict:
    splits = jax.random.split(jax.random.key(seed), 5)
    return {
        "traits": gaussian(splits[0], (NSUB, K), 1.0, 6.0, ((0, 32), (1, 16))),
        "kin_tiles": gaussian(splits[1], (NTILES, BLOCK, BLOCK), (2 * BLOCK) ** -0.5, 0.25, ((0, 32),)),
        "kin_index": draw_kin_index(jax.random.fold_in(splits[4], 71), 0),
        "dosages": draw_dosages(jax.random.fold_in(splits[4], 71), 0),
    }


def kinship_apply(field, kin_tiles, kin_index):
    width = field.shape[1]
    slabs = field.reshape(NBLOCKS, BLOCK, width)[kin_index[:, 1]].astype(jnp.float32)
    prods = jnp.einsum('tij,tjk->tik', kin_tiles.astype(jnp.float32), slabs)
    summed = jax.ops.segment_sum(prods, kin_index[:, 0], NBLOCKS)
    return summed.reshape(NSUB, width)

def reference(traits, kin_tiles, kin_index, dosages):
    first = kinship_apply(traits, kin_tiles, kin_index)
    first_sent = first.astype(jnp.bfloat16)
    second = kinship_apply(first_sent, kin_tiles, kin_index)
    base = traits.astype(jnp.float32)
    whitened = (0.6 * base + 0.5 * first + 0.3 * (2.0 * second - base)).astype(jnp.bfloat16)
    scale = 1.0 / (127.5 * jnp.sqrt(jnp.float32(NSUB)))
    blocks = dosages.reshape(NSUB, N_VAR, VAR_DEV).transpose(1, 0, 2)

    def score_block(block_dos):
        return lax.dot_general(block_dos, whitened, (((0,), (0,)), ((), ())), preferred_element_type=jnp.float32)
    scores = lax.map(score_block, blocks).reshape(NVAR, K)
    return scores * scale
```

```python
import functools

import jax
import jax.numpy as jnp
from jax import lax
from jax.experimental import pallas as pl
from jax.experimental.pallas import tpu as pltpu
from jax.sharding import PartitionSpec as P

NEAR = 4
LANES = 128
VMEM = pl.BlockSpec(memory_space=pltpu.VMEM)
SMEM = pl.BlockSpec(memory_space=pltpu.SMEM)
PARAMS = pltpu.CompilerParams(vmem_limit_bytes=48 * 2**20)


def list_kernel(slots, here, index_ref, out_ref):
    me = lax.axis_index("subj")
    lane = lax.broadcasted_iota(jnp.int32, out_ref.shape[1:], 1)
    row = jnp.full(lane.shape, -1, jnp.int32)
    count = jnp.int32(0)
    for t in range(index_ref.shape[0]):
        col = index_ref[t, 1]
        remote = col // here != me
        row = jnp.where((lane == count) & remote, col, row)
        count = count + remote.astype(jnp.int32)
    for k in range(out_ref.shape[0]):
        out_ref[k] = row


def pack_kernel(slots, here, block, wanted_ref, near_ref, out_ref):
    group = lax.axis_index("subj") // NEAR
    for k in range(out_ref.shape[0]):
        for j in range(slots):
            col = wanted_ref[k, 0, j]

            @pl.when((col >= 0) & (col // (here * NEAR) == group))
            def _(k=k, j=j, col=col):
                inside = col - group * (here * NEAR)
                at = pl.multiple_of(inside % here * block, block)
                out_ref[k, j] = near_ref[inside // here, :, pl.ds(at, block)]


def apply_tiles(slots, here, block, index_ref, field_ref, far_ref, tiles_ref, sum_ref):
    me = lax.axis_index("subj")
    sum_ref[...] = jnp.zeros_like(sum_ref)
    count = jnp.int32(0)
    for t in range(tiles_ref.shape[0]):
        row = index_ref[t, 0] - me * here
        col = index_ref[t, 1]
        local = col // here == me
        at = pl.multiple_of(col % here * block, block)
        mine = field_ref[:, pl.ds(at, block)]
        other = far_ref[col // (here * NEAR), jnp.minimum(count, slots - 1)]
        count = count + jnp.where(local, 0, 1)
        slab = jnp.where(local, mine, other)
        prod = lax.dot_general(
            slab, tiles_ref[t], (((1,), (1,)), ((), ())), preferred_element_type=jnp.float32
        )
        to = pl.ds(pl.multiple_of(row * block, block), block)
        sum_ref[:, to] += prod


def first_kernel(slots, here, block, index_ref, field_ref, far_ref, tiles_ref, sum_ref, sent_ref):
    apply_tiles(slots, here, block, index_ref, field_ref, far_ref, tiles_ref, sum_ref)
    sent_ref[...] = sum_ref[...].astype(sent_ref.dtype)


def second_kernel(
    slots, here, block, index_ref, sent_ref, far_ref, tiles_ref, first_ref, traits_ref, out_ref, sum_ref
):
    apply_tiles(slots, here, block, index_ref, sent_ref, far_ref, tiles_ref, sum_ref)
    base = traits_ref[...].astype(jnp.float32)
    whitened = 0.6 * base + 0.5 * first_ref[...] + 0.3 * (2.0 * sum_ref[...] - base)
    whitened = whitened.astype(out_ref.dtype)
    for k in range(out_ref.shape[0]):
        out_ref[k] = whitened


def score_kernel(scale, wide_ref, dosages_ref, out_ref):
    cores, chips, rows, width = out_ref.shape
    step = 256
    for i in range(dosages_ref.shape[1] // step):
        part = jnp.dot(
            wide_ref[...], dosages_ref[:, i * step : (i + 1) * step], preferred_element_type=jnp.float32
        )
        part = part.T * scale
        for r in range(0, step, 8):
            at = i * step + r
            owner, inner = at // rows, at % rows
            out_ref[owner % cores, owner // cores, inner : inner + 8, :] = part[r : r + 8]


def add_kernel(mine_ref, other_ref, out_ref):
    out_ref[...] = mine_ref[...] + other_ref[...]


def sum_kernel(parts_ref, out_ref):
    total = parts_ref[0]
    for k in range(1, parts_ref.shape[0]):
        total = total + parts_ref[k]
    out_ref[...] = total


def call(kernel, out, specs, scratch=()):
    many = isinstance(out, list)
    return pl.pallas_call(
        kernel,
        out_shape=out,
        in_specs=specs,
        out_specs=[VMEM] * len(out) if many else VMEM,
        scratch_shapes=list(scratch),
        compiler_params=PARAMS,
    )


def on_device(traits, kin_tiles, kin_index, dosages):
    n = lax.axis_size("subj")
    m = lax.axis_size("var")
    rows_here, width = traits.shape
    tiles, block = kin_tiles.shape[:2]
    here = rows_here // block
    slots = tiles - here
    far = n // NEAR
    near_groups = [[k * NEAR + j for j in range(NEAR)] for k in range(far)]
    far_groups = [[k * NEAR + j for k in range(far)] for j in range(NEAR)]
    chip_groups = [list(range(c, n, 2)) for c in range(2)]
    f32, bf16 = jnp.float32, jnp.bfloat16
    sds = jax.ShapeDtypeStruct
    base = traits.T

    listed = call(
        functools.partial(list_kernel, slots, here), sds((far, 8, LANES), jnp.int32), [SMEM]
    )(kin_index)
    wanted = lax.all_to_all(listed, "subj", 0, 0, tiled=True, axis_index_groups=far_groups)
    wanted = wanted[:, :1, :8]

    def fetched(field):
        near = lax.all_gather(field, "subj", axis_index_groups=near_groups)
        packed = call(
            functools.partial(pack_kernel, slots, here, block),
            sds((far, slots, width, block), bf16),
            [SMEM, VMEM],
        )(wanted, near)
        return lax.all_to_all(packed, "subj", 0, 0, tiled=True, axis_index_groups=far_groups)

    first, sent = call(
        functools.partial(first_kernel, slots, here, block),
        [sds((width, rows_here), f32), sds((width, rows_here), bf16)],
        [SMEM, VMEM, VMEM, VMEM],
    )(kin_index, base, fetched(base), kin_tiles)
    copies = call(
        functools.partial(second_kernel, slots, here, block),
        sds((m, width, rows_here), bf16),
        [SMEM, VMEM, VMEM, VMEM, VMEM, VMEM],
        [pltpu.VMEM((width, rows_here), f32)],
    )(kin_index, sent, fetched(sent), kin_tiles, first, base)
    wide = lax.all_to_all(copies, "var", 0, 0, tiled=True).reshape(m * width, rows_here)

    scale = 1.0 / (127.5 * float(rows_here * n) ** 0.5)
    share = dosages.shape[1] // n
    parts = call(
        functools.partial(score_kernel, scale),
        sds((2, n // 2, share, m * width), f32),
        [VMEM, VMEM],
    )(wide, dosages)
    core = lax.axis_index("subj") % 2
    mine = lax.dynamic_index_in_dim(parts, core, 0, keepdims=False)
    other = lax.dynamic_index_in_dim(parts, 1 - core, 0, keepdims=False)
    other = lax.ppermute(other, "subj", [(s, s ^ 1) for s in range(n)])
    half = call(add_kernel, sds(mine.shape, f32), [VMEM, VMEM])(mine, other)
    arrived = lax.all_to_all(half, "subj", 0, 0, tiled=True, axis_index_groups=chip_groups)
    return call(sum_kernel, sds((share, m * width), f32), [VMEM])(arrived)


def solution(mesh):
    in_specs = (P("subj", "var"), P("subj", None, None), P("subj", None), P("subj", "var"))
    out_specs = P(("var", "subj"), None)
    return jax.shard_map(
        on_device, mesh=mesh, in_specs=in_specs, out_specs=out_specs, check_vma=False
    )
```

```python
import functools

import jax
import jax.numpy as jnp
from jax import lax
from jax.experimental import pallas as pl
from jax.experimental.pallas import tpu as pltpu
from jax.sharding import PartitionSpec as P

NEAR = 4
LANES = 128
NONE = 256
VMEM = pl.BlockSpec(memory_space=pltpu.VMEM)
ANY = pl.BlockSpec(memory_space=pl.ANY)
SMEM = pl.BlockSpec(memory_space=pltpu.SMEM)
PARAMS = pltpu.CompilerParams(vmem_limit_bytes=48 * 2**20)


def send_kernel(here, index_ref, field_ref, out_ref):
    me = lax.axis_index("subj")
    rows_here = field_ref.shape[1]
    shape = (field_ref.shape[0], out_ref.shape[2] - rows_here)
    lane = lax.broadcasted_iota(jnp.int32, shape, 1)
    listed = jnp.full(shape, NONE, jnp.int32)
    count = jnp.int32(0)
    for t in range(index_ref.shape[1]):
        col = index_ref[1, t]
        remote = jnp.where(col // here != me, 1, 0)
        listed = jnp.where(lane == jnp.where(remote == 1, count, -1), col, listed)
        count = count + remote
    listed = listed.astype(jnp.float32).astype(out_ref.dtype)
    for k in range(out_ref.shape[0]):
        out_ref[k, :, :rows_here] = field_ref[...]
        out_ref[k, :, rows_here:] = listed


def pack_near_kernel(slots, here, block, index_ref, far_ref, out_ref):
    me = lax.axis_index("subj")
    group, inner = me // NEAR, me % NEAR
    for p in range(NEAR):
        count = jnp.int32(0)
        for t in range(index_ref.shape[2]):
            col = index_ref[p, 1, t]
            owner = col // here
            remote = owner != group * NEAR + p

            @pl.when(remote & (owner % NEAR == inner))
            def _(p=p, col=col, owner=owner, count=count):
                at = pl.multiple_of(col % here * block, block)
                out_ref[p, jnp.minimum(count, slots - 1)] = far_ref[owner // NEAR, :, pl.ds(at, block)]

            count = count + jnp.where(remote, 1, 0)


def pack_far_kernel(slots, here, block, wanted_ref, near_ref, out_ref):
    group = lax.axis_index("subj") // NEAR
    for k in range(out_ref.shape[0]):
        for j in range(slots):
            col = wanted_ref[k, j]

            @pl.when((col < NONE) & (col // (here * NEAR) == group))
            def _(k=k, j=j, col=col):
                inside = col - group * (here * NEAR)
                at = pl.multiple_of(inside % here * block, block)
                out_ref[k, j] = near_ref[inside // here, :, pl.ds(at, block)]


def apply_tiles(slots, here, block, source, index_ref, field_ref, other_ref, tile, sum_ref):
    me = lax.axis_index("subj")
    inner = me % NEAR
    sum_ref[...] = jnp.zeros_like(sum_ref)
    count = jnp.int32(0)
    for t in range(index_ref.shape[2]):
        row = index_ref[inner, 0, t] - me * here
        col = index_ref[inner, 1, t]
        local = col // here == me
        at = pl.multiple_of(col % here * block, block)
        mine = field_ref[:, pl.ds(at, block)]
        other = other_ref[source(col), jnp.minimum(count, slots - 1)]
        count = count + jnp.where(local, 0, 1)
        slab = jnp.where(local, mine, other)
        prod = lax.dot_general(
            slab, tile(t), (((1,), (1,)), ((), ())), preferred_element_type=jnp.float32
        )
        to = pl.ds(pl.multiple_of(row * block, block), block)
        sum_ref[:, to] += prod


def first_kernel(
    slots, here, block, index_ref, far_ref, other_ref, tiles_ref, sum_ref, sent_ref, held, sems
):
    copies = [
        pltpu.make_async_copy(tiles_ref.at[t], held.at[t], sems.at[t]) for t in range(held.shape[0])
    ]
    for copy in copies:
        copy.start()

    def tile(t):
        copies[t].wait()
        return held[t]

    def source(col):
        return col // here % NEAR

    own = far_ref.at[lax.axis_index("subj") // NEAR]
    apply_tiles(slots, here, block, source, index_ref, own, other_ref, tile, sum_ref)
    sent_ref[...] = sum_ref[...].astype(sent_ref.dtype)


def second_kernel(
    slots, here, block, index_ref, sent_ref, other_ref, tiles_ref, first_ref, far_ref, out_ref, sum_ref
):
    def source(col):
        return col // (here * NEAR)

    def tile(t):
        return tiles_ref[t]

    apply_tiles(slots, here, block, source, index_ref, sent_ref, other_ref, tile, sum_ref)
    rows_here = sum_ref.shape[1]
    base = far_ref[lax.axis_index("subj") // NEAR, :, :rows_here].astype(jnp.float32)
    whitened = 0.6 * base + 0.5 * first_ref[...] + 0.3 * (2.0 * sum_ref[...] - base)
    whitened = whitened.astype(out_ref.dtype)
    for k in range(out_ref.shape[0]):
        out_ref[k] = whitened


def score_kernel(scale, wide_ref, dosages_ref, out_ref, held, sems):
    core = lax.axis_index("subj") % 2
    rows = out_ref.shape[2]
    steps, _, step = held.shape
    copies = [
        pltpu.make_async_copy(
            dosages_ref.at[:, i * step : (i + 1) * step], held.at[i], sems.at[i]
        )
        for i in range(steps)
    ]
    for copy in copies:
        copy.start()
    for i in range(steps):
        copies[i].wait()
        part = jnp.dot(wide_ref[...], held[i], preferred_element_type=jnp.float32)
        part = part.T * scale
        for r in range(0, step, 8):
            owner, inner = divmod(i * step + r, rows)
            out_ref[core if owner % 2 == 0 else 1 - core, owner // 2, inner : inner + 8, :] = part[r : r + 8]


def add_kernel(mine_ref, other_ref, out_ref):
    out_ref[...] = mine_ref[...] + other_ref[...]


def sum_kernel(parts_ref, out_ref):
    total = parts_ref[0]
    for k in range(1, parts_ref.shape[0]):
        total = total + parts_ref[k]
    out_ref[...] = total


def call(kernel, out, specs, scratch=()):
    many = isinstance(out, list)
    return pl.pallas_call(
        kernel,
        out_shape=out,
        in_specs=specs,
        out_specs=[VMEM] * len(out) if many else VMEM,
        scratch_shapes=list(scratch),
        compiler_params=PARAMS,
    )


def on_device(traits, kin_tiles, kin_index, dosages):
    n = lax.axis_size("subj")
    m = lax.axis_size("var")
    rows_here, width = traits.shape
    tiles, block = kin_tiles.shape[:2]
    here = rows_here // block
    slots = tiles - here
    far = n // NEAR
    near_groups = [[k * NEAR + j for j in range(NEAR)] for k in range(far)]
    far_groups = [[k * NEAR + j for k in range(far)] for j in range(NEAR)]
    chip_groups = [list(range(c, n, 2)) for c in range(2)]
    f32, bf16 = jnp.float32, jnp.bfloat16
    sds = jax.ShapeDtypeStruct
    base = traits.T
    index = kin_index.T

    out = call(
        functools.partial(send_kernel, here), sds((far, width, rows_here + LANES), bf16), [SMEM, VMEM]
    )(index, base)
    dense = lax.all_to_all(out, "subj", 0, 0, tiled=True, axis_index_groups=far_groups)
    near_index = lax.all_gather(index, "subj", axis_index_groups=near_groups)
    wanted = dense[:, 0, rows_here : rows_here + slots].astype(jnp.int32)
    packed = call(
        functools.partial(pack_near_kernel, slots, here, block),
        sds((NEAR, slots, width, block), bf16),
        [SMEM, VMEM],
    )(near_index, dense)
    arrived = lax.all_to_all(packed, "subj", 0, 0, tiled=True, axis_index_groups=near_groups)
    first, sent = call(
        functools.partial(first_kernel, slots, here, block),
        [sds((width, rows_here), f32), sds((width, rows_here), bf16)],
        [SMEM, VMEM, VMEM, ANY],
        [pltpu.VMEM(kin_tiles.shape, bf16), pltpu.SemaphoreType.DMA((tiles,))],
    )(near_index, dense, arrived, kin_tiles)

    near = lax.all_gather(sent, "subj", axis_index_groups=near_groups)
    packed = call(
        functools.partial(pack_far_kernel, slots, here, block),
        sds((far, slots, width, block), bf16),
        [SMEM, VMEM],
    )(wanted, near)
    arrived = lax.all_to_all(packed, "subj", 0, 0, tiled=True, axis_index_groups=far_groups)
    copies = call(
        functools.partial(second_kernel, slots, here, block),
        sds((m, width, rows_here), bf16),
        [SMEM, VMEM, VMEM, VMEM, VMEM, VMEM],
        [pltpu.VMEM((width, rows_here), f32)],
    )(near_index, sent, arrived, kin_tiles, first, dense)
    wide = lax.all_to_all(copies, "var", 0, 0, tiled=True).reshape(m * width, rows_here)

    scale = 1.0 / (127.5 * float(rows_here * n) ** 0.5)
    share = dosages.shape[1] // n
    step = 256
    parts = call(
        functools.partial(score_kernel, scale),
        sds((2, n // 2, share, m * width), f32),
        [VMEM, ANY],
        [
            pltpu.VMEM((dosages.shape[1] // step, rows_here, step), bf16),
            pltpu.SemaphoreType.DMA((dosages.shape[1] // step,)),
        ],
    )(wide, dosages)
    mine = parts[0]
    other = lax.ppermute(parts[1], "subj", [(s, s ^ 1) for s in range(n)])
    half = call(add_kernel, sds(mine.shape, f32), [VMEM, VMEM])(mine, other)
    arrived = lax.all_to_all(half, "subj", 0, 0, tiled=True, axis_index_groups=chip_groups)
    return call(sum_kernel, sds((share, m * width), f32), [VMEM])(arrived)


def solution(mesh):
    in_specs = (P("subj", "var"), P("subj", None, None), P("subj", None), P("subj", "var"))
    out_specs = P(("var", "subj"), None)
    return jax.shard_map(
        on_device, mesh=mesh, in_specs=in_specs, out_specs=out_specs, check_vma=False
    )
```

```python
import functools

import jax
import jax.numpy as jnp
from jax import lax
from jax.experimental import pallas as pl
from jax.experimental.pallas import tpu as pltpu
from jax.sharding import PartitionSpec as P

NEAR_TRAITS, NEAR_FIRST = 8, 4
LANES = 128
NONE = -1
VMEM = pl.BlockSpec(memory_space=pltpu.VMEM)
SMEM = pl.BlockSpec(memory_space=pltpu.SMEM)
PARAMS = pltpu.CompilerParams(vmem_limit_bytes=48 * 2**20)


def list_kernel(here, index_ref, out_ref):
    me = lax.axis_index("subj")
    shape = out_ref.shape[1:]
    lane = lax.broadcasted_iota(jnp.int32, shape, 1)
    line = lax.broadcasted_iota(jnp.int32, shape, 0)
    listed = jnp.full(shape, NONE, jnp.int32)
    count = jnp.int32(0)
    for t in range(index_ref.shape[1]):
        row, col = index_ref[0, t], index_ref[1, t]
        remote = jnp.where(col // here != me, 1, 0)
        listed = jnp.where((line == 0) & (lane == jnp.where(remote == 1, count, -1)), col, listed)
        listed = jnp.where((line == 1) & (lane == t), row, listed)
        listed = jnp.where((line == 2) & (lane == t), col, listed)
        count = count + remote
    for k in range(out_ref.shape[0]):
        out_ref[k] = listed


def pack_kernel(group, here, block, lists_ref, near_ref, out_ref):
    me = lax.axis_index("subj")
    near = near_ref.shape[0]
    for k in range(out_ref.shape[0]):
        partner = (k * near + me % near) // group
        for j in range(out_ref.shape[1]):
            col = lists_ref[partner, 0, j]

            @pl.when((col >= 0) & (col // (here * near) == me // near))
            def _(k=k, j=j, col=col):
                inside = col - me // near * (here * near)
                at = pl.multiple_of(inside % here * block, block)
                out_ref[k, j] = near_ref[inside // here, :, pl.ds(at, block)]


def apply_tiles(group, here, block, lists_ref, field_ref, other_ref, tiles_ref, sum_ref):
    me = lax.axis_index("subj")
    sources, slots = other_ref.shape[:2]
    held = lax.axis_size("subj") // sources * here
    sum_ref[...] = jnp.zeros_like(sum_ref)
    count = jnp.int32(0)
    for t in range(tiles_ref.shape[0]):
        row = lists_ref[me // group, 1, t] - me * here
        col = lists_ref[me // group, 2, t]
        local = col // here == me
        at = pl.multiple_of(col % here * block, block)
        mine = field_ref[:, pl.ds(at, block)]
        other = other_ref[col // held, jnp.minimum(count, slots - 1)]
        count = count + jnp.where(local, 0, 1)
        slab = jnp.where(local, mine, other)
        prod = lax.dot_general(
            slab, tiles_ref[t], (((1,), (1,)), ((), ())), preferred_element_type=jnp.float32
        )
        to = pl.ds(pl.multiple_of(row * block, block), block)
        sum_ref[:, to] += prod


def first_kernel(
    group, here, block, lists_ref, near_ref, other_ref, tiles_ref, sum_ref, sent_ref
):
    own = near_ref.at[lax.axis_index("subj") % near_ref.shape[0]]
    apply_tiles(group, here, block, lists_ref, own, other_ref, tiles_ref, sum_ref)
    sent_ref[...] = sum_ref[...].astype(sent_ref.dtype)


def second_kernel(
    group, here, block, lists_ref, sent_ref, other_ref, tiles_ref, first_ref, near_ref, out_ref, sum_ref
):
    apply_tiles(group, here, block, lists_ref, sent_ref, other_ref, tiles_ref, sum_ref)
    base = near_ref[lax.axis_index("subj") % near_ref.shape[0]].astype(jnp.float32)
    whitened = 0.6 * base + 0.5 * first_ref[...] + 0.3 * (2.0 * sum_ref[...] - base)
    whitened = whitened.astype(out_ref.dtype)
    for k in range(out_ref.shape[0]):
        out_ref[k] = whitened


def score_kernel(scale, wide_ref, dosages_ref, out_ref):
    core = lax.axis_index("subj") % 2
    rows = out_ref.shape[2]
    step = 256
    for i in range(dosages_ref.shape[1] // step):
        part = jnp.dot(
            wide_ref[...], dosages_ref[:, i * step : (i + 1) * step], preferred_element_type=jnp.float32
        )
        part = part.T * scale
        for r in range(0, step, 8):
            owner, inner = divmod(i * step + r, rows)
            out_ref[core if owner % 2 == 0 else 1 - core, owner // 2, inner : inner + 8, :] = part[r : r + 8]


def add_kernel(mine_ref, other_ref, out_ref):
    rows, lanes = mine_ref.shape[1], out_ref.shape[2]
    for i in range(out_ref.shape[1] // rows):
        part = slice(i * lanes, (i + 1) * lanes)
        out_ref[:, i * rows : (i + 1) * rows, :] = (mine_ref[:, :, part] + other_ref[:, :, part]).astype(out_ref.dtype)


def sum_kernel(parts_ref, out_ref):
    total = parts_ref[0].astype(jnp.float32)
    for k in range(1, parts_ref.shape[0]):
        total = total + parts_ref[k].astype(jnp.float32)
    rows, lanes = out_ref.shape[0], parts_ref.shape[2]
    for i in range(out_ref.shape[1] // lanes):
        out_ref[:, i * lanes : (i + 1) * lanes] = total[i * rows : (i + 1) * rows]


def call(kernel, out, specs, scratch=()):
    many = isinstance(out, list)
    return pl.pallas_call(
        kernel,
        out_shape=out,
        in_specs=specs,
        out_specs=[VMEM] * len(out) if many else VMEM,
        scratch_shapes=list(scratch),
        compiler_params=PARAMS,
    )


def on_device(traits, kin_tiles, kin_index, dosages):
    n = lax.axis_size("subj")
    m = lax.axis_size("var")
    rows_here, width = traits.shape
    tiles, block = kin_tiles.shape[:2]
    here = rows_here // block
    slots = tiles - here
    lists = n // NEAR_FIRST
    chip_groups = [list(range(c, n, 2)) for c in range(2)]
    f32, bf16 = jnp.float32, jnp.bfloat16
    sds = jax.ShapeDtypeStruct

    def far_groups(near):
        return [list(range(i, n, near)) for i in range(near)]

    def gathered(field, near):
        groups = [list(range(k, k + near)) for k in range(0, n, near)]
        return lax.all_gather(field, "subj", axis_index_groups=groups)

    def fetched(lists, field):
        near = field.shape[0]
        packed = call(
            functools.partial(pack_kernel, NEAR_FIRST, here, block),
            sds((n // near, slots, width, block), bf16),
            [SMEM, VMEM],
        )(lists, field)
        return lax.all_to_all(packed, "subj", 0, 0, tiled=True, axis_index_groups=far_groups(near))

    listed = call(
        functools.partial(list_kernel, here), sds((lists, 8, LANES), jnp.int32), [SMEM]
    )(kin_index.T)
    listed = lax.all_to_all(
        listed, "subj", 0, 0, tiled=True, axis_index_groups=far_groups(NEAR_FIRST)
    )
    listed = listed[:, :3, :tiles]
    near = gathered(traits.T, NEAR_TRAITS)
    first, sent = call(
        functools.partial(first_kernel, NEAR_FIRST, here, block),
        [sds((width, rows_here), f32), sds((width, rows_here), bf16)],
        [SMEM, VMEM, VMEM, VMEM],
    )(listed, near, fetched(listed, near), kin_tiles)
    copies = call(
        functools.partial(second_kernel, NEAR_FIRST, here, block),
        sds((m, width, rows_here), bf16),
        [SMEM, VMEM, VMEM, VMEM, VMEM, VMEM],
        [pltpu.VMEM((width, rows_here), f32)],
    )(listed, sent, fetched(listed, gathered(sent, NEAR_FIRST)), kin_tiles, first, near)
    wide = lax.all_to_all(copies, "var", 0, 0, tiled=True).reshape(m * width, rows_here)

    scale = 1.0 / (127.5 * float(rows_here * n) ** 0.5)
    share = dosages.shape[1] // n
    parts = call(
        functools.partial(score_kernel, scale),
        sds((2, n // 2, share, m * width), f32),
        [VMEM, VMEM],
    )(wide, dosages)
    mine = parts[0]
    other = lax.ppermute(parts[1], "subj", [(s, s ^ 1) for s in range(n)])
    half = sds((n // 2, share * m * width // LANES, LANES), bf16)
    half = call(add_kernel, half, [VMEM, VMEM])(mine, other)
    arrived = lax.all_to_all(half, "subj", 0, 0, tiled=True, axis_index_groups=chip_groups)
    return call(sum_kernel, sds((share, m * width), f32), [VMEM])(arrived)


def solution(mesh):
    in_specs = (P("subj", "var"), P("subj", None, None), P("subj", None), P("subj", "var"))
    out_specs = P(("var", "subj"), None)
    return jax.shard_map(
        on_device, mesh=mesh, in_specs=in_specs, out_specs=out_specs, check_vma=False
    )
```

```python
import functools

import jax
import jax.numpy as jnp
from jax import lax
from jax.experimental import pallas as pl
from jax.experimental.pallas import tpu as pltpu
from jax.sharding import PartitionSpec as P

NEAR = 4
LANES = 128
NONE = -1
VMEM = pl.BlockSpec(memory_space=pltpu.VMEM)
SMEM = pl.BlockSpec(memory_space=pltpu.SMEM)


def list_kernel(here, index_ref, out_ref):
    me = lax.axis_index("subj")
    shape = out_ref.shape[1:]
    lane = lax.broadcasted_iota(jnp.int32, shape, 1)
    line = lax.broadcasted_iota(jnp.int32, shape, 0)
    listed = jnp.full(shape, NONE, jnp.int32)
    count = jnp.int32(0)
    for t in range(index_ref.shape[1]):
        row, col = index_ref[0, t], index_ref[1, t]
        remote = jnp.where(col // here != me, 1, 0)
        listed = jnp.where((line == 0) & (lane == jnp.where(remote == 1, count, -1)), col, listed)
        listed = jnp.where((line == 1) & (lane == t), row, listed)
        listed = jnp.where((line == 2) & (lane == t), col, listed)
        count = count + remote
    for k in range(out_ref.shape[0]):
        out_ref[k] = listed


def pack_kernel(here, block, lists_ref, near_ref, out_ref):
    first = lax.axis_index("subj") // NEAR * (NEAR * here)
    for k in range(out_ref.shape[0]):
        for j in range(out_ref.shape[1]):
            inside = jnp.clip(lists_ref[k, 0, j] - first, 0, NEAR * here - 1)
            at = pl.multiple_of(inside % here * block, block)
            out_ref[k, j] = near_ref[inside // here, :, pl.ds(at, block)]


def apply_tiles(here, block, lists_ref, field_ref, other_ref, tiles_ref, sum_ref):
    me = lax.axis_index("subj")
    slots = other_ref.shape[1]
    sum_ref[...] = jnp.zeros_like(sum_ref)
    count = jnp.int32(0)
    for t in range(tiles_ref.shape[0]):
        row = lists_ref[me // NEAR, 1, t] - me * here
        col = lists_ref[me // NEAR, 2, t]
        local = col // here == me
        at = pl.multiple_of(col % here * block, block)
        mine = field_ref[:, pl.ds(at, block)]
        other = other_ref[col // (here * NEAR), jnp.minimum(count, slots - 1)]
        count = count + jnp.where(local, 0, 1)
        slab = jnp.where(local, mine, other)
        prod = lax.dot_general(
            slab, tiles_ref[t], (((1,), (1,)), ((), ())), preferred_element_type=jnp.float32
        )
        to = pl.ds(pl.multiple_of(row * block, block), block)
        sum_ref[:, to] += prod


def first_kernel(
    here, block, lists_ref, near_ref, other_ref, tiles_ref, sum_ref, sent_ref
):
    own = near_ref.at[lax.axis_index("subj") % NEAR]
    apply_tiles(here, block, lists_ref, own, other_ref, tiles_ref, sum_ref)
    sent_ref[...] = sum_ref[...].astype(sent_ref.dtype)


def second_kernel(
    here, block, lists_ref, sent_ref, other_ref, tiles_ref, first_ref, near_ref, out_ref, sum_ref
):
    apply_tiles(here, block, lists_ref, sent_ref, other_ref, tiles_ref, sum_ref)
    base = near_ref[lax.axis_index("subj") % NEAR].astype(jnp.float32)
    whitened = 0.6 * base + 0.5 * first_ref[...] + 0.3 * (2.0 * sum_ref[...] - base)
    whitened = whitened.astype(out_ref.dtype)
    for k in range(out_ref.shape[0]):
        out_ref[k] = whitened


def score_kernel(scale, wide_ref, dosages_ref, out_ref):
    core = lax.axis_index("subj") % 2
    rows = out_ref.shape[2]
    step = 256
    for i in range(dosages_ref.shape[1] // step):
        part = jnp.dot(
            wide_ref[...], dosages_ref[:, i * step : (i + 1) * step], preferred_element_type=jnp.float32
        )
        part = part.T * scale
        for r in range(0, step, 8):
            owner, inner = divmod(i * step + r, rows)
            to = core if owner % 2 == 0 else 1 - core
            out_ref[to, owner // 2, inner : inner + 8, :] = part[r : r + 8]


def add_kernel(parts_ref, both_ref, out_ref):
    other = 1 - lax.axis_index("subj") % 2
    rows, lanes = parts_ref.shape[2], out_ref.shape[2]
    for i in range(out_ref.shape[1] // rows):
        part = slice(i * lanes, (i + 1) * lanes)
        total = parts_ref[0, :, :, part] + both_ref[other, :, :, part]
        out_ref[:, i * rows : (i + 1) * rows, :] = total.astype(out_ref.dtype)


def sum_kernel(parts_ref, out_ref):
    total = parts_ref[0].astype(jnp.float32)
    for k in range(1, parts_ref.shape[0]):
        total = total + parts_ref[k].astype(jnp.float32)
    rows, lanes = out_ref.shape[0], parts_ref.shape[2]
    for i in range(out_ref.shape[1] // lanes):
        out_ref[:, i * lanes : (i + 1) * lanes] = total[i * rows : (i + 1) * rows]


def call(kernel, out, specs, scratch=(), mib=48):
    many = isinstance(out, list)
    return pl.pallas_call(
        kernel,
        out_shape=out,
        in_specs=specs,
        out_specs=[VMEM] * len(out) if many else VMEM,
        scratch_shapes=list(scratch),
        compiler_params=pltpu.CompilerParams(vmem_limit_bytes=mib * 2**20),
    )


def on_device(traits, kin_tiles, kin_index, dosages):
    n = lax.axis_size("subj")
    m = lax.axis_size("var")
    rows_here, width = traits.shape
    tiles, block = kin_tiles.shape[:2]
    here = rows_here // block
    slots = tiles - here
    far = n // NEAR
    near_groups = [list(range(k, k + NEAR)) for k in range(0, n, NEAR)]
    far_groups = [list(range(i, n, NEAR)) for i in range(NEAR)]
    chip_groups = [list(range(c, n, 2)) for c in range(2)]
    core_groups = [[s, s + 1] for s in range(0, n, 2)]
    f32, bf16 = jnp.float32, jnp.bfloat16
    sds = jax.ShapeDtypeStruct

    def exchanged(x, groups):
        return lax.all_to_all(x, "subj", 0, 0, tiled=True, axis_index_groups=groups)

    def gathered(field):
        return lax.all_gather(field, "subj", axis_index_groups=near_groups)

    def fetched(lists, near):
        packed = call(
            functools.partial(pack_kernel, here, block),
            sds((far, slots, width, block), bf16),
            [SMEM, VMEM],
        )(lists, near)
        return exchanged(packed, far_groups)

    lists = call(
        functools.partial(list_kernel, here), sds((far, 8, LANES), jnp.int32), [SMEM], mib=62
    )(kin_index.T)
    lists = exchanged(lists, far_groups)[:, :3, :tiles]
    near = gathered(traits.T)
    first, sent = call(
        functools.partial(first_kernel, here, block),
        [sds((width, rows_here), f32), sds((width, rows_here), bf16)],
        [SMEM, VMEM, VMEM, VMEM],
    )(lists, near, fetched(lists, near), kin_tiles)
    copies = call(
        functools.partial(second_kernel, here, block),
        sds((m, width, rows_here), bf16),
        [SMEM, VMEM, VMEM, VMEM, VMEM, VMEM],
        [pltpu.VMEM((width, rows_here), f32)],
    )(lists, sent, fetched(lists, gathered(sent)), kin_tiles, first, near)
    wide = lax.all_to_all(copies, "var", 0, 0, tiled=True).reshape(m * width, rows_here)

    scale = 1.0 / (127.5 * float(rows_here * n) ** 0.5)
    share = dosages.shape[1] // n
    parts = sds((2, n // 2, share, m * width), f32)
    parts = call(functools.partial(score_kernel, scale), parts, [VMEM, VMEM])(wide, dosages)
    both = lax.all_gather(parts[1], "subj", axis_index_groups=core_groups)
    half = sds((n // 2, share * m * width // LANES, LANES), bf16)
    half = call(add_kernel, half, [VMEM, VMEM])(parts, both)
    arrived = exchanged(half, chip_groups)
    return call(sum_kernel, sds((share, m * width), f32), [VMEM])(arrived)


def solution(mesh):
    in_specs = (P("subj", "var"), P("subj", None, None), P("subj", None), P("subj", "var"))
    out_specs = P(("var", "subj"), None)
    return jax.shard_map(
        on_device, mesh=mesh, in_specs=in_specs, out_specs=out_specs, check_vma=False
    )
```

```python
import functools

import jax
import jax.numpy as jnp
from jax import lax
from jax.experimental import pallas as pl
from jax.experimental.pallas import tpu as pltpu
from jax.sharding import PartitionSpec as P

NEAR = 4
LANES = 128
TURN, VAR_TURN = 5, 15
NONE = -1
VMEM = pl.BlockSpec(memory_space=pltpu.VMEM)
HBM = pl.BlockSpec(memory_space=pltpu.HBM)
SMEM = pl.BlockSpec(memory_space=pltpu.SMEM)


def turned(group, turn):
    return group[turn:] + group[:turn]


def place(k, size, turn):
    return (k + size - turn) % size


def list_kernel(here, index_ref, out_ref):
    me = lax.axis_index("subj")
    shape = out_ref.shape[1:]
    lane = lax.broadcasted_iota(jnp.int32, shape, 1)
    line = lax.broadcasted_iota(jnp.int32, shape, 0)
    listed = jnp.full(shape, NONE, jnp.int32)
    count = jnp.int32(0)
    for t in range(index_ref.shape[1]):
        row, col = index_ref[0, t], index_ref[1, t]
        remote = jnp.where(col // here != me, 1, 0)
        slot = lane == jnp.where(remote == 1, count, -1)
        listed = jnp.where((line == 0) & slot, col, listed)
        listed = jnp.where((line == 3) & slot, t, listed)
        listed = jnp.where((line == 1) & (lane == t), row, listed)
        listed = jnp.where((line == 2) & (lane == t), col, listed)
        count = count + remote
    for k in range(out_ref.shape[0]):
        out_ref[k] = listed


def pack_kernel(here, block, lists_ref, near_ref, out_ref):
    first = lax.axis_index("subj") // NEAR * (NEAR * here)
    for k in range(out_ref.shape[0]):
        for j in range(out_ref.shape[1]):
            inside = jnp.clip(lists_ref[k, 0, j] - first, 0, NEAR * here - 1)
            at = pl.multiple_of(inside % here * block, block)
            out_ref[k, j] = near_ref[inside // here, :, pl.ds(at, block)]


def tile_dot(slab, tile):
    return lax.dot_general(slab, tile, (((1,), (1,)), ((), ())), preferred_element_type=jnp.float32)


def apply_tiles(here, block, lists_ref, field_ref, other_ref, tiles_ref, sum_ref):
    me = lax.axis_index("subj")
    far, slots = other_ref.shape[:2]
    mine = place(me // NEAR, far, TURN)
    sum_ref[...] = jnp.zeros_like(sum_ref)
    count = jnp.int32(0)
    for t in range(tiles_ref.shape[0]):
        row = lists_ref[mine, 1, t] - me * here
        col = lists_ref[mine, 2, t]
        local = col // here == me
        at = pl.multiple_of(col % here * block, block)
        own = field_ref[:, pl.ds(at, block)]
        other = other_ref[place(col // (here * NEAR), far, TURN), jnp.minimum(count, slots - 1)]
        count = count + jnp.where(local, 0, 1)
        slab = jnp.where(local, own, other)
        prod = tile_dot(slab, tiles_ref[t])
        to = pl.ds(pl.multiple_of(row * block, block), block)
        sum_ref[:, to] += prod


def local_kernel(here, block, lists_ref, near_ref, tiles_ref, sum_ref, held_ref, sem):
    me = lax.axis_index("subj")
    mine = place(me // NEAR, lists_ref.shape[0], TURN)
    copy = pltpu.make_async_copy(tiles_ref, held_ref, sem)
    copy.start()
    sum_ref[...] = jnp.zeros_like(sum_ref)
    copy.wait()
    for t in range(held_ref.shape[0]):
        row = lists_ref[mine, 1, t] - me * here
        col = lists_ref[mine, 2, t]
        at = pl.multiple_of(col % here * block, block)
        slab = near_ref[me % NEAR, :, pl.ds(at, block)]
        slab = jnp.where(col // here == me, slab, jnp.zeros_like(slab))
        to = pl.ds(pl.multiple_of(row * block, block), block)
        sum_ref[:, to] += tile_dot(slab, held_ref[t])


def first_kernel(here, block, lists_ref, local_ref, other_ref, tiles_ref, sum_ref, sent_ref):
    me = lax.axis_index("subj")
    far = lists_ref.shape[0]
    mine = place(me // NEAR, far, TURN)
    sum_ref[...] = local_ref[...]
    for j in range(other_ref.shape[1]):
        col = lists_ref[mine, 0, j]
        t = jnp.maximum(lists_ref[mine, 3, j], 0)
        row = lists_ref[mine, 1, t] - me * here
        slab = other_ref[place(jnp.maximum(col, 0) // (here * NEAR), far, TURN), j]
        slab = jnp.where(col >= 0, slab, jnp.zeros_like(slab))
        to = pl.ds(pl.multiple_of(row * block, block), block)
        sum_ref[:, to] += tile_dot(slab, tiles_ref[t])
    sent_ref[...] = sum_ref[...].astype(sent_ref.dtype)


def second_kernel(
    here, block, lists_ref, sent_ref, other_ref, tiles_ref, first_ref, near_ref, out_ref, sum_ref
):
    apply_tiles(here, block, lists_ref, sent_ref, other_ref, tiles_ref, sum_ref)
    base = near_ref[lax.axis_index("subj") % NEAR].astype(jnp.float32)
    whitened = 0.6 * base + 0.5 * first_ref[...] + 0.3 * (2.0 * sum_ref[...] - base)
    whitened = whitened.astype(out_ref.dtype)
    for k in range(out_ref.shape[0]):
        out_ref[k] = whitened


def score_kernel(scale, width, wide_ref, dosages_ref, out_ref):
    core = lax.axis_index("subj") % 2
    rows = out_ref.shape[2]
    step = 256
    top = wide_ref.shape[0] - VAR_TURN * width
    wide = jnp.concatenate([wide_ref[top:], wide_ref[:top]])
    for i in range(dosages_ref.shape[1] // step):
        part = jnp.dot(
            wide, dosages_ref[:, i * step : (i + 1) * step], preferred_element_type=jnp.float32
        )
        part = part.T * scale
        for r in range(0, step, 8):
            owner, inner = divmod(i * step + r, rows)
            to = core if owner % 2 == 0 else 1 - core
            out_ref[to, place(owner // 2, out_ref.shape[1], 2 * TURN), inner : inner + 8, :] = part[r : r + 8]


def add_kernel(parts_ref, both_ref, out_ref):
    other = 1 - lax.axis_index("subj") % 2
    rows, lanes = parts_ref.shape[2], out_ref.shape[2]
    for i in range(out_ref.shape[1] // rows):
        part = slice(i * lanes, (i + 1) * lanes)
        total = parts_ref[0, :, :, part] + both_ref[other, :, :, part]
        out_ref[:, i * rows : (i + 1) * rows, :] = total.astype(out_ref.dtype)


def sum_kernel(parts_ref, out_ref):
    total = parts_ref[0].astype(jnp.float32)
    for k in range(1, parts_ref.shape[0]):
        total = total + parts_ref[k].astype(jnp.float32)
    rows, lanes = out_ref.shape[0], parts_ref.shape[2]
    for i in range(out_ref.shape[1] // lanes):
        out_ref[:, i * lanes : (i + 1) * lanes] = total[i * rows : (i + 1) * rows]


def call(kernel, out, specs, scratch=(), mib=48):
    many = isinstance(out, list)
    return pl.pallas_call(
        kernel,
        out_shape=out,
        in_specs=specs,
        out_specs=[VMEM] * len(out) if many else VMEM,
        scratch_shapes=list(scratch),
        compiler_params=pltpu.CompilerParams(vmem_limit_bytes=mib * 2**20),
    )


def on_device(traits, kin_tiles, kin_index, dosages):
    n = lax.axis_size("subj")
    m = lax.axis_size("var")
    rows_here, width = traits.shape
    tiles, block = kin_tiles.shape[:2]
    here = rows_here // block
    slots = tiles - here
    far = n // NEAR
    near_groups = [list(range(k, k + NEAR)) for k in range(0, n, NEAR)]
    far_groups = [turned(list(range(i, n, NEAR)), TURN) for i in range(NEAR)]
    chip_groups = [turned(list(range(c, n, 2)), 2 * TURN) for c in range(2)]
    var_groups = [turned(list(range(m)), VAR_TURN)]
    core_groups = [[s, s + 1] for s in range(0, n, 2)]
    f32, bf16 = jnp.float32, jnp.bfloat16
    sds = jax.ShapeDtypeStruct

    def exchanged(x, groups):
        return lax.all_to_all(x, "subj", 0, 0, tiled=True, axis_index_groups=groups)

    def gathered(field):
        return lax.all_gather(field, "subj", axis_index_groups=near_groups)

    def fetched(lists, near):
        packed = call(
            functools.partial(pack_kernel, here, block),
            sds((far, slots, width, block), bf16),
            [SMEM, VMEM],
        )(lists, near)
        return exchanged(packed, far_groups)

    lists = call(
        functools.partial(list_kernel, here), sds((far, 8, LANES), jnp.int32), [SMEM], mib=62
    )(kin_index.T)
    lists = exchanged(lists, far_groups)[:, :4, :tiles]
    near = gathered(traits.T)
    local, held = call(
        functools.partial(local_kernel, here, block),
        [sds((width, rows_here), f32), sds(kin_tiles.shape, bf16)],
        [SMEM, VMEM, HBM],
        [pltpu.SemaphoreType.DMA],
    )(lists, near, kin_tiles)
    first, sent = call(
        functools.partial(first_kernel, here, block),
        [sds((width, rows_here), f32), sds((width, rows_here), bf16)],
        [SMEM, VMEM, VMEM, VMEM],
    )(lists, local, fetched(lists, near), held)
    copies = call(
        functools.partial(second_kernel, here, block),
        sds((m, width, rows_here), bf16),
        [SMEM, VMEM, VMEM, VMEM, VMEM, VMEM],
        [pltpu.VMEM((width, rows_here), f32)],
    )(lists, sent, fetched(lists, gathered(sent)), held, first, near)
    wide = lax.all_to_all(copies, "var", 0, 0, tiled=True, axis_index_groups=var_groups)
    wide = wide.reshape(m * width, rows_here)

    scale = 1.0 / (127.5 * float(rows_here * n) ** 0.5)
    share = dosages.shape[1] // n
    parts = sds((2, n // 2, share, m * width), f32)
    parts = call(functools.partial(score_kernel, scale, width), parts, [VMEM, VMEM])(wide, dosages)
    both = lax.all_gather(parts[1], "subj", axis_index_groups=core_groups)
    half = sds((n // 2, share * m * width // LANES, LANES), bf16)
    half = call(add_kernel, half, [VMEM, VMEM])(parts, both)
    arrived = exchanged(half, chip_groups)
    return call(sum_kernel, sds((share, m * width), f32), [VMEM])(arrived)


def solution(mesh):
    in_specs = (P("subj", "var"), P("subj", None, None), P("subj", None), P("subj", "var"))
    out_specs = P(("var", "subj"), None)
    return jax.shard_map(
        on_device, mesh=mesh, in_specs=in_specs, out_specs=out_specs, check_vma=False
    )
```

```python
import functools

import jax
import jax.numpy as jnp
from jax import lax
from jax.experimental import pallas as pl
from jax.experimental.pallas import tpu as pltpu
from jax.sharding import PartitionSpec as P

NEAR = 4
LANES = 128
LIST_TURN, TRAIT_TURN, FIRST_TURN, VAR_TURN = 5, 4, 4, 15
CHIP_TURN = 8
NONE = -1
VMEM = pl.BlockSpec(memory_space=pltpu.VMEM)
HBM = pl.BlockSpec(memory_space=pltpu.HBM)
SMEM = pl.BlockSpec(memory_space=pltpu.SMEM)


def turned(group, turn):
    return group[turn:] + group[:turn]


def place(k, size, turn):
    return (k + size - turn) % size


def list_kernel(here, index_ref, out_ref):
    me = lax.axis_index("subj")
    shape = out_ref.shape[1:]
    lane = lax.broadcasted_iota(jnp.int32, shape, 1)
    line = lax.broadcasted_iota(jnp.int32, shape, 0)
    listed = jnp.full(shape, NONE, jnp.int32)
    count = jnp.int32(0)
    for t in range(index_ref.shape[1]):
        row, col = index_ref[0, t], index_ref[1, t]
        remote = jnp.where(col // here != me, 1, 0)
        slot = lane == jnp.where(remote == 1, count, -1)
        listed = jnp.where((line == 0) & slot, col, listed)
        listed = jnp.where((line == 3) & slot, t, listed)
        listed = jnp.where((line == 1) & (lane == t), row, listed)
        listed = jnp.where((line == 2) & (lane == t), col, listed)
        count = count + remote
    for k in range(out_ref.shape[0]):
        out_ref[k] = listed


def pack_kernel(here, block, turn, lists_ref, near_ref, out_ref):
    first = lax.axis_index("subj") // NEAR * (NEAR * here)
    far = out_ref.shape[0]
    for k in range(far):
        listed = place(k + turn, far, LIST_TURN)
        for j in range(out_ref.shape[1]):
            inside = jnp.clip(lists_ref[listed, 0, j] - first, 0, NEAR * here - 1)
            at = pl.multiple_of(inside % here * block, block)
            out_ref[k, j] = near_ref[inside // here, :, pl.ds(at, block)]


def tile_dot(slab, tile):
    return lax.dot_general(slab, tile, (((1,), (1,)), ((), ())), preferred_element_type=jnp.float32)


def apply_tiles(here, block, lists_ref, field_ref, other_ref, tiles_ref, sum_ref):
    me = lax.axis_index("subj")
    far, slots = other_ref.shape[:2]
    mine = place(me // NEAR, far, LIST_TURN)
    sum_ref[...] = jnp.zeros_like(sum_ref)
    count = jnp.int32(0)
    for t in range(tiles_ref.shape[0]):
        row = lists_ref[mine, 1, t] - me * here
        col = lists_ref[mine, 2, t]
        local = col // here == me
        at = pl.multiple_of(col % here * block, block)
        own = field_ref[:, pl.ds(at, block)]
        other = other_ref[place(col // (here * NEAR), far, FIRST_TURN), jnp.minimum(count, slots - 1)]
        count = count + jnp.where(local, 0, 1)
        slab = jnp.where(local, own, other)
        prod = tile_dot(slab, tiles_ref[t])
        to = pl.ds(pl.multiple_of(row * block, block), block)
        sum_ref[:, to] += prod


def local_kernel(here, block, lists_ref, near_ref, tiles_ref, sum_ref, held_ref, sem):
    me = lax.axis_index("subj")
    mine = place(me // NEAR, lists_ref.shape[0], LIST_TURN)
    copy = pltpu.make_async_copy(tiles_ref, held_ref, sem)
    copy.start()
    sum_ref[...] = jnp.zeros_like(sum_ref)
    copy.wait()
    for t in range(held_ref.shape[0]):
        row = lists_ref[mine, 1, t] - me * here
        col = lists_ref[mine, 2, t]
        at = pl.multiple_of(col % here * block, block)
        slab = near_ref[me % NEAR, :, pl.ds(at, block)]
        slab = jnp.where(col // here == me, slab, jnp.zeros_like(slab))
        to = pl.ds(pl.multiple_of(row * block, block), block)
        sum_ref[:, to] += tile_dot(slab, held_ref[t])


def first_kernel(here, block, lists_ref, local_ref, other_ref, tiles_ref, sum_ref, sent_ref):
    me = lax.axis_index("subj")
    far = lists_ref.shape[0]
    mine = place(me // NEAR, far, LIST_TURN)
    sum_ref[...] = local_ref[...]
    for j in range(other_ref.shape[1]):
        col = lists_ref[mine, 0, j]
        t = jnp.maximum(lists_ref[mine, 3, j], 0)
        row = lists_ref[mine, 1, t] - me * here
        slab = other_ref[place(jnp.maximum(col, 0) // (here * NEAR), far, TRAIT_TURN), j]
        slab = jnp.where(col >= 0, slab, jnp.zeros_like(slab))
        to = pl.ds(pl.multiple_of(row * block, block), block)
        sum_ref[:, to] += tile_dot(slab, tiles_ref[t])
    sent_ref[...] = sum_ref[...].astype(sent_ref.dtype)


def second_kernel(
    here, block, lists_ref, sent_ref, other_ref, tiles_ref, first_ref, near_ref, out_ref, sum_ref
):
    apply_tiles(here, block, lists_ref, sent_ref, other_ref, tiles_ref, sum_ref)
    base = near_ref[lax.axis_index("subj") % NEAR].astype(jnp.float32)
    whitened = 0.6 * base + 0.5 * first_ref[...] + 0.3 * (2.0 * sum_ref[...] - base)
    whitened = whitened.astype(out_ref.dtype)
    for k in range(out_ref.shape[0]):
        out_ref[k] = whitened


def score_kernel(scale, width, wide_ref, dosages_ref, out_ref):
    core = lax.axis_index("subj") % 2
    rows = out_ref.shape[2]
    step = 256
    top = wide_ref.shape[0] - VAR_TURN * width
    wide = jnp.concatenate([wide_ref[top:], wide_ref[:top]])
    for i in range(dosages_ref.shape[1] // step):
        part = jnp.dot(
            wide, dosages_ref[:, i * step : (i + 1) * step], preferred_element_type=jnp.float32
        )
        part = part.T * scale
        for r in range(0, step, 8):
            owner, inner = divmod(i * step + r, rows)
            to = core if owner % 2 == 0 else 1 - core
            out_ref[to, place(owner // 2, out_ref.shape[1], CHIP_TURN), inner : inner + 8, :] = part[r : r + 8]


def add_kernel(parts_ref, both_ref, out_ref):
    other = 1 - lax.axis_index("subj") % 2
    rows, lanes = parts_ref.shape[2], out_ref.shape[2]
    for i in range(out_ref.shape[1] // rows):
        part = slice(i * lanes, (i + 1) * lanes)
        total = parts_ref[0, :, :, part] + both_ref[other, :, :, part]
        out_ref[:, i * rows : (i + 1) * rows, :] = total.astype(out_ref.dtype)


def sum_kernel(parts_ref, out_ref):
    total = parts_ref[0].astype(jnp.float32)
    for k in range(1, parts_ref.shape[0]):
        total = total + parts_ref[k].astype(jnp.float32)
    rows, lanes = out_ref.shape[0], parts_ref.shape[2]
    for i in range(out_ref.shape[1] // lanes):
        out_ref[:, i * lanes : (i + 1) * lanes] = total[i * rows : (i + 1) * rows]


def call(kernel, out, specs, scratch=(), mib=48):
    many = isinstance(out, list)
    return pl.pallas_call(
        kernel,
        out_shape=out,
        in_specs=specs,
        out_specs=[VMEM] * len(out) if many else VMEM,
        scratch_shapes=list(scratch),
        compiler_params=pltpu.CompilerParams(vmem_limit_bytes=mib * 2**20),
    )


def on_device(traits, kin_tiles, kin_index, dosages):
    n = lax.axis_size("subj")
    m = lax.axis_size("var")
    rows_here, width = traits.shape
    tiles, block = kin_tiles.shape[:2]
    here = rows_here // block
    slots = tiles - here
    far = n // NEAR
    near_groups = [list(range(k, k + NEAR)) for k in range(0, n, NEAR)]
    chip_groups = [turned(list(range(c, n, 2)), CHIP_TURN) for c in range(2)]
    var_groups = [turned(list(range(m)), VAR_TURN)]
    core_groups = [[s, s + 1] for s in range(0, n, 2)]
    f32, bf16 = jnp.float32, jnp.bfloat16
    sds = jax.ShapeDtypeStruct

    def far_groups(turn):
        return [turned(list(range(i, n, NEAR)), turn) for i in range(NEAR)]

    def exchanged(x, groups):
        return lax.all_to_all(x, "subj", 0, 0, tiled=True, axis_index_groups=groups)

    def gathered(field):
        return lax.all_gather(field, "subj", axis_index_groups=near_groups)

    def fetched(lists, near, turn):
        packed = call(
            functools.partial(pack_kernel, here, block, turn),
            sds((far, slots, width, block), bf16),
            [SMEM, VMEM],
        )(lists, near)
        return exchanged(packed, far_groups(turn))

    lists = call(
        functools.partial(list_kernel, here), sds((far, 8, LANES), jnp.int32), [SMEM], mib=62
    )(kin_index.T)
    lists = exchanged(lists, far_groups(LIST_TURN))[:, :4, :tiles]
    near = gathered(traits.T)
    local, held = call(
        functools.partial(local_kernel, here, block),
        [sds((width, rows_here), f32), sds(kin_tiles.shape, bf16)],
        [SMEM, VMEM, HBM],
        [pltpu.SemaphoreType.DMA],
    )(lists, near, kin_tiles)
    first, sent = call(
        functools.partial(first_kernel, here, block),
        [sds((width, rows_here), f32), sds((width, rows_here), bf16)],
        [SMEM, VMEM, VMEM, VMEM],
    )(lists, local, fetched(lists, near, TRAIT_TURN), held)
    copies = call(
        functools.partial(second_kernel, here, block),
        sds((m, width, rows_here), bf16),
        [SMEM, VMEM, VMEM, VMEM, VMEM, VMEM],
        [pltpu.VMEM((width, rows_here), f32)],
    )(lists, sent, fetched(lists, gathered(sent), FIRST_TURN), held, first, near)
    wide = lax.all_to_all(copies, "var", 0, 0, tiled=True, axis_index_groups=var_groups)
    wide = wide.reshape(m * width, rows_here)

    scale = 1.0 / (127.5 * float(rows_here * n) ** 0.5)
    share = dosages.shape[1] // n
    parts = sds((2, n // 2, share, m * width), f32)
    parts = call(functools.partial(score_kernel, scale, width), parts, [VMEM, VMEM])(wide, dosages)
    both = lax.all_gather(parts[1], "subj", axis_index_groups=core_groups)
    half = sds((n // 2, share * m * width // LANES, LANES), bf16)
    half = call(add_kernel, half, [VMEM, VMEM])(parts, both)
    arrived = exchanged(half, chip_groups)
    return call(sum_kernel, sds((share, m * width), f32), [VMEM])(arrived)


def solution(mesh):
    in_specs = (P("subj", "var"), P("subj", None, None), P("subj", None), P("subj", "var"))
    out_specs = P(("var", "subj"), None)
    return jax.shard_map(
        on_device, mesh=mesh, in_specs=in_specs, out_specs=out_specs, check_vma=False
    )
```

```python
import functools

import jax
import jax.numpy as jnp
from jax import lax
from jax.experimental import pallas as pl
from jax.experimental.pallas import tpu as pltpu
from jax.sharding import PartitionSpec as P

NEAR = 4
LANES = 128
LIST_TURN, TRAIT_TURN, FIRST_TURN, VAR_TURN = 6, 4, 4, 15
CHIP_TURN = 8
NONE = -1
VMEM = pl.BlockSpec(memory_space=pltpu.VMEM)
HBM = pl.BlockSpec(memory_space=pltpu.HBM)
SMEM = pl.BlockSpec(memory_space=pltpu.SMEM)


def turned(group, turn):
    return group[turn:] + group[:turn]


def place(k, size, turn):
    return (k + size - turn) % size


def list_kernel(here, index_ref, out_ref):
    me = lax.axis_index("subj")
    shape = out_ref.shape[1:]
    lane = lax.broadcasted_iota(jnp.int32, shape, 1)
    line = lax.broadcasted_iota(jnp.int32, shape, 0)
    listed = jnp.full(shape, NONE, jnp.int32)
    count = jnp.int32(0)
    for t in range(index_ref.shape[1]):
        row, col = index_ref[0, t], index_ref[1, t]
        remote = jnp.where(col // here != me, 1, 0)
        slot = lane == jnp.where(remote == 1, count, -1)
        listed = jnp.where((line == 0) & slot, col, listed)
        listed = jnp.where((line == 3) & slot, t, listed)
        listed = jnp.where((line == 1) & (lane == t), row, listed)
        listed = jnp.where((line == 2) & (lane == t), col, listed)
        count = count + remote
    for k in range(out_ref.shape[0]):
        out_ref[k] = listed


def pack_kernel(here, block, turn, lists_ref, near_ref, out_ref):
    first = lax.axis_index("subj") // NEAR * (NEAR * here)
    far = out_ref.shape[0]
    for k in range(far):
        listed = place(k + turn, far, LIST_TURN)
        for j in range(out_ref.shape[1]):
            inside = jnp.clip(lists_ref[listed, 0, j] - first, 0, NEAR * here - 1)
            at = pl.multiple_of(inside % here * block, block)
            out_ref[k, j] = near_ref[inside // here, :, pl.ds(at, block)]


def tile_dot(slab, tile):
    return lax.dot_general(slab, tile, (((1,), (1,)), ((), ())), preferred_element_type=jnp.float32)


def apply_tiles(here, block, lists_ref, field_ref, other_ref, tiles_ref, sum_ref):
    me = lax.axis_index("subj")
    far, slots = other_ref.shape[:2]
    mine = place(me // NEAR, far, LIST_TURN)
    sum_ref[...] = jnp.zeros_like(sum_ref)
    count = jnp.int32(0)
    for t in range(tiles_ref.shape[0]):
        row = lists_ref[mine, 1, t] - me * here
        col = lists_ref[mine, 2, t]
        local = col // here == me
        at = pl.multiple_of(col % here * block, block)
        own = field_ref[:, pl.ds(at, block)]
        other = other_ref[place(col // (here * NEAR), far, FIRST_TURN), jnp.minimum(count, slots - 1)]
        count = count + jnp.where(local, 0, 1)
        slab = jnp.where(local, own, other)
        prod = tile_dot(slab, tiles_ref[t])
        to = pl.ds(pl.multiple_of(row * block, block), block)
        sum_ref[:, to] += prod


def local_kernel(here, block, lists_ref, near_ref, tiles_ref, sum_ref, held_ref, sem):
    me = lax.axis_index("subj")
    mine = place(me // NEAR, lists_ref.shape[0], LIST_TURN)
    copy = pltpu.make_async_copy(tiles_ref, held_ref, sem)
    copy.start()
    sum_ref[...] = jnp.zeros_like(sum_ref)
    copy.wait()
    for t in range(held_ref.shape[0]):
        row = lists_ref[mine, 1, t] - me * here
        col = lists_ref[mine, 2, t]
        at = pl.multiple_of(col % here * block, block)
        slab = near_ref[me % NEAR, :, pl.ds(at, block)]
        slab = jnp.where(col // here == me, slab, jnp.zeros_like(slab))
        to = pl.ds(pl.multiple_of(row * block, block), block)
        sum_ref[:, to] += tile_dot(slab, held_ref[t])


def first_kernel(here, block, lists_ref, local_ref, other_ref, tiles_ref, sum_ref, sent_ref):
    me = lax.axis_index("subj")
    far = lists_ref.shape[0]
    mine = place(me // NEAR, far, LIST_TURN)
    sum_ref[...] = local_ref[...]
    for j in range(other_ref.shape[1]):
        col = lists_ref[mine, 0, j]
        t = jnp.maximum(lists_ref[mine, 3, j], 0)
        row = lists_ref[mine, 1, t] - me * here
        slab = other_ref[place(jnp.maximum(col, 0) // (here * NEAR), far, TRAIT_TURN), j]
        slab = jnp.where(col >= 0, slab, jnp.zeros_like(slab))
        to = pl.ds(pl.multiple_of(row * block, block), block)
        sum_ref[:, to] += tile_dot(slab, tiles_ref[t])
    sent_ref[...] = sum_ref[...].astype(sent_ref.dtype)


def second_kernel(
    here, block, lists_ref, sent_ref, other_ref, tiles_ref, first_ref, near_ref, out_ref, sum_ref
):
    apply_tiles(here, block, lists_ref, sent_ref, other_ref, tiles_ref, sum_ref)
    base = near_ref[lax.axis_index("subj") % NEAR].astype(jnp.float32)
    whitened = 0.6 * base + 0.5 * first_ref[...] + 0.3 * (2.0 * sum_ref[...] - base)
    whitened = whitened.astype(out_ref.dtype)
    for k in range(out_ref.shape[0]):
        out_ref[k] = whitened


def score_kernel(scale, width, wide_ref, dosages_ref, out_ref):
    core = lax.axis_index("subj") % 2
    rows = out_ref.shape[2]
    step = 256
    top = wide_ref.shape[0] - VAR_TURN * width
    wide = jnp.concatenate([wide_ref[top:], wide_ref[:top]])
    for i in range(dosages_ref.shape[1] // step):
        part = jnp.dot(
            wide, dosages_ref[:, i * step : (i + 1) * step], preferred_element_type=jnp.float32
        )
        part = part.T * scale
        for r in range(0, step, 8):
            owner, inner = divmod(i * step + r, rows)
            to = core if owner % 2 == 0 else 1 - core
            out_ref[to, place(owner // 2, out_ref.shape[1], CHIP_TURN), inner : inner + 8, :] = part[r : r + 8]


def add_kernel(parts_ref, both_ref, out_ref):
    other = 1 - lax.axis_index("subj") % 2
    rows, lanes = parts_ref.shape[2], out_ref.shape[2]
    for i in range(out_ref.shape[1] // rows):
        part = slice(i * lanes, (i + 1) * lanes)
        total = parts_ref[0, :, :, part] + both_ref[other, :, :, part]
        out_ref[:, i * rows : (i + 1) * rows, :] = total.astype(out_ref.dtype)


def sum_kernel(parts_ref, out_ref):
    total = parts_ref[0].astype(jnp.float32)
    for k in range(1, parts_ref.shape[0]):
        total = total + parts_ref[k].astype(jnp.float32)
    rows, lanes = out_ref.shape[0], parts_ref.shape[2]
    for i in range(out_ref.shape[1] // lanes):
        out_ref[:, i * lanes : (i + 1) * lanes] = total[i * rows : (i + 1) * rows]


def call(kernel, out, specs, scratch=(), mib=48):
    many = isinstance(out, list)
    return pl.pallas_call(
        kernel,
        out_shape=out,
        in_specs=specs,
        out_specs=[VMEM] * len(out) if many else VMEM,
        scratch_shapes=list(scratch),
        compiler_params=pltpu.CompilerParams(vmem_limit_bytes=mib * 2**20),
    )


def on_device(traits, kin_tiles, kin_index, dosages):
    n = lax.axis_size("subj")
    m = lax.axis_size("var")
    rows_here, width = traits.shape
    tiles, block = kin_tiles.shape[:2]
    here = rows_here // block
    slots = tiles - here
    far = n // NEAR
    near_groups = [list(range(k, k + NEAR)) for k in range(0, n, NEAR)]
    chip_groups = [turned(list(range(c, n, 2)), CHIP_TURN) for c in range(2)]
    var_groups = [turned(list(range(m)), VAR_TURN)]
    core_groups = [[s, s + 1] for s in range(0, n, 2)]
    f32, bf16 = jnp.float32, jnp.bfloat16
    sds = jax.ShapeDtypeStruct

    def far_groups(turn):
        return [turned(list(range(i, n, NEAR)), turn) for i in range(NEAR)]

    def exchanged(x, groups):
        return lax.all_to_all(x, "subj", 0, 0, tiled=True, axis_index_groups=groups)

    def gathered(field):
        return lax.all_gather(field, "subj", axis_index_groups=near_groups)

    def fetched(lists, near, turn):
        packed = call(
            functools.partial(pack_kernel, here, block, turn),
            sds((far, slots, width, block), bf16),
            [SMEM, VMEM],
        )(lists, near)
        return exchanged(packed, far_groups(turn))

    lists = call(
        functools.partial(list_kernel, here), sds((far, 8, LANES), jnp.int32), [SMEM], mib=62
    )(kin_index.T)
    lists = exchanged(lists, far_groups(LIST_TURN))[:, :4, :tiles]
    near = gathered(traits.T)
    local, held = call(
        functools.partial(local_kernel, here, block),
        [sds((width, rows_here), f32), sds(kin_tiles.shape, bf16)],
        [SMEM, VMEM, HBM],
        [pltpu.SemaphoreType.DMA],
    )(lists, near, kin_tiles)
    first, sent = call(
        functools.partial(first_kernel, here, block),
        [sds((width, rows_here), f32), sds((width, rows_here), bf16)],
        [SMEM, VMEM, VMEM, VMEM],
    )(lists, local, fetched(lists, near, TRAIT_TURN), held)
    copies = call(
        functools.partial(second_kernel, here, block),
        sds((m, width, rows_here), bf16),
        [SMEM, VMEM, VMEM, VMEM, VMEM, VMEM],
        [pltpu.VMEM((width, rows_here), f32)],
    )(lists, sent, fetched(lists, gathered(sent), FIRST_TURN), held, first, near)
    wide = lax.all_to_all(copies, "var", 0, 0, tiled=True, axis_index_groups=var_groups)
    wide = wide.reshape(m * width, rows_here)

    scale = 1.0 / (127.5 * float(rows_here * n) ** 0.5)
    share = dosages.shape[1] // n
    parts = sds((2, n // 2, share, m * width), f32)
    parts = call(functools.partial(score_kernel, scale, width), parts, [VMEM, VMEM])(wide, dosages)
    both = lax.all_gather(parts[1], "subj", axis_index_groups=core_groups)
    half = sds((n // 2, share * m * width // LANES, LANES), bf16)
    half = call(add_kernel, half, [VMEM, VMEM])(parts, both)
    arrived = exchanged(half, chip_groups)
    return call(sum_kernel, sds((share, m * width), f32), [VMEM])(arrived)


def solution(mesh):
    in_specs = (P("subj", "var"), P("subj", None, None), P("subj", None), P("subj", "var"))
    out_specs = P(("var", "subj"), None)
    return jax.shard_map(
        on_device, mesh=mesh, in_specs=in_specs, out_specs=out_specs, check_vma=False
    )
```

```python
import functools

import jax
import jax.numpy as jnp
from jax import lax
from jax.experimental import pallas as pl
from jax.experimental.pallas import tpu as pltpu
from jax.sharding import PartitionSpec as P

NEAR = 4
LANES = 128
LIST_TURN, TRAIT_TURN, FIRST_TURN, VAR_TURN = 6, 4, 4, 15
CHIP_TURN = 8
NONE = -1
VMEM = pl.BlockSpec(memory_space=pltpu.VMEM)
HBM = pl.BlockSpec(memory_space=pltpu.HBM)
SMEM = pl.BlockSpec(memory_space=pltpu.SMEM)


def turned(group, turn):
    return group[turn:] + group[:turn]


def place(k, size, turn):
    return (k + size - turn) % size


def list_kernel(here, index_ref, out_ref):
    me = lax.axis_index("subj")
    shape = out_ref.shape[1:]
    lane = lax.broadcasted_iota(jnp.int32, shape, 1)
    line = lax.broadcasted_iota(jnp.int32, shape, 0)
    listed = jnp.full(shape, NONE, jnp.int32)
    count = jnp.int32(0)
    for t in range(index_ref.shape[1]):
        row, col = index_ref[0, t], index_ref[1, t]
        remote = jnp.where(col // here != me, 1, 0)
        slot = lane == jnp.where(remote == 1, count, -1)
        listed = jnp.where((line == 0) & slot, col, listed)
        listed = jnp.where((line == 3) & slot, t, listed)
        listed = jnp.where((line == 1) & (lane == t), row, listed)
        listed = jnp.where((line == 2) & (lane == t), col, listed)
        count = count + remote
    for k in range(out_ref.shape[0]):
        out_ref[k] = listed


def pack_kernel(here, block, turn, lists_ref, near_ref, out_ref):
    first = lax.axis_index("subj") // NEAR * (NEAR * here)
    far = out_ref.shape[0]
    for k in range(far):
        listed = place(k + turn, far, LIST_TURN)
        for j in range(out_ref.shape[1]):
            inside = jnp.clip(lists_ref[listed, 0, j] - first, 0, NEAR * here - 1)
            at = pl.multiple_of(inside % here * block, block)
            out_ref[k, j] = near_ref[inside // here, :, pl.ds(at, block)]


def tile_dot(slab, tile):
    return lax.dot_general(slab, tile, (((1,), (1,)), ((), ())), preferred_element_type=jnp.float32)


def apply_tiles(here, block, lists_ref, field_ref, other_ref, tiles_ref, sum_ref):
    me = lax.axis_index("subj")
    far, slots = other_ref.shape[:2]
    mine = place(me // NEAR, far, LIST_TURN)
    sum_ref[...] = jnp.zeros_like(sum_ref)
    count = jnp.int32(0)
    for t in range(tiles_ref.shape[0]):
        row = lists_ref[mine, 1, t] - me * here
        col = lists_ref[mine, 2, t]
        local = col // here == me
        at = pl.multiple_of(col % here * block, block)
        own = field_ref[:, pl.ds(at, block)]
        other = other_ref[place(col // (here * NEAR), far, FIRST_TURN), jnp.minimum(count, slots - 1)]
        count = count + jnp.where(local, 0, 1)
        slab = jnp.where(local, own, other)
        prod = tile_dot(slab, tiles_ref[t])
        to = pl.ds(pl.multiple_of(row * block, block), block)
        sum_ref[:, to] += prod


def local_kernel(here, block, lists_ref, near_ref, tiles_ref, sum_ref, held_ref, sem):
    me = lax.axis_index("subj")
    mine = place(me // NEAR, lists_ref.shape[0], LIST_TURN)
    copy = pltpu.make_async_copy(tiles_ref, held_ref, sem)
    copy.start()
    sum_ref[...] = jnp.zeros_like(sum_ref)
    copy.wait()
    for t in range(held_ref.shape[0]):
        row = lists_ref[mine, 1, t] - me * here
        col = lists_ref[mine, 2, t]
        at = pl.multiple_of(col % here * block, block)
        slab = near_ref[me % NEAR, :, pl.ds(at, block)]
        slab = jnp.where(col // here == me, slab, jnp.zeros_like(slab))
        to = pl.ds(pl.multiple_of(row * block, block), block)
        sum_ref[:, to] += tile_dot(slab, held_ref[t])


def first_kernel(here, block, lists_ref, local_ref, other_ref, tiles_ref, sum_ref, sent_ref):
    me = lax.axis_index("subj")
    far = lists_ref.shape[0]
    mine = place(me // NEAR, far, LIST_TURN)
    sum_ref[...] = local_ref[...]
    for j in range(other_ref.shape[1]):
        col = lists_ref[mine, 0, j]
        t = jnp.maximum(lists_ref[mine, 3, j], 0)
        row = lists_ref[mine, 1, t] - me * here
        slab = other_ref[place(jnp.maximum(col, 0) // (here * NEAR), far, TRAIT_TURN), j]
        slab = jnp.where(col >= 0, slab, jnp.zeros_like(slab))
        to = pl.ds(pl.multiple_of(row * block, block), block)
        sum_ref[:, to] += tile_dot(slab, tiles_ref[t])
    sent_ref[...] = sum_ref[...].astype(sent_ref.dtype)


def second_kernel(
    here, block, lists_ref, sent_ref, other_ref, tiles_ref, first_ref, near_ref, out_ref, sum_ref
):
    apply_tiles(here, block, lists_ref, sent_ref, other_ref, tiles_ref, sum_ref)
    base = near_ref[lax.axis_index("subj") % NEAR].astype(jnp.float32)
    whitened = 0.6 * base + 0.5 * first_ref[...] + 0.3 * (2.0 * sum_ref[...] - base)
    whitened = whitened.astype(out_ref.dtype)
    for k in range(out_ref.shape[0]):
        out_ref[k] = whitened


def score_kernel(scale, width, wide_ref, dosages_ref, out_ref):
    core = lax.axis_index("subj") % 2
    rows = out_ref.shape[2]
    step = 256
    top = wide_ref.shape[0] - VAR_TURN * width
    wide = jnp.concatenate([wide_ref[top:], wide_ref[:top]])
    for i in range(dosages_ref.shape[1] // step):
        part = jnp.dot(
            wide, dosages_ref[:, i * step : (i + 1) * step], preferred_element_type=jnp.float32
        )
        part = part.T * scale
        for r in range(0, step, 8):
            owner, inner = divmod(i * step + r, rows)
            to = core if owner % 2 == 0 else 1 - core
            out_ref[to, place(owner // 2, out_ref.shape[1], CHIP_TURN), inner : inner + 8, :] = part[r : r + 8]


def add_kernel(parts_ref, both_ref, out_ref):
    other = 1 - lax.axis_index("subj") % 2
    lanes = out_ref.shape[2]
    total = parts_ref[0] + both_ref[other]
    halves = [total[:, :, i : i + lanes] for i in range(0, total.shape[2], lanes)]
    out_ref[...] = jnp.concatenate(halves, axis=1).astype(out_ref.dtype)


def sum_kernel(parts_ref, out_ref):
    total = parts_ref[0].astype(jnp.float32)
    for k in range(1, parts_ref.shape[0]):
        total = total + parts_ref[k].astype(jnp.float32)
    rows, lanes = out_ref.shape[0], parts_ref.shape[2]
    for i in range(out_ref.shape[1] // lanes):
        out_ref[:, i * lanes : (i + 1) * lanes] = total[i * rows : (i + 1) * rows]


def call(kernel, out, specs, scratch=(), mib=48):
    many = isinstance(out, list)
    return pl.pallas_call(
        kernel,
        out_shape=out,
        in_specs=specs,
        out_specs=[VMEM] * len(out) if many else VMEM,
        scratch_shapes=list(scratch),
        compiler_params=pltpu.CompilerParams(vmem_limit_bytes=mib * 2**20),
    )


def on_device(traits, kin_tiles, kin_index, dosages):
    n = lax.axis_size("subj")
    m = lax.axis_size("var")
    rows_here, width = traits.shape
    tiles, block = kin_tiles.shape[:2]
    here = rows_here // block
    slots = tiles - here
    far = n // NEAR
    near_groups = [list(range(k, k + NEAR)) for k in range(0, n, NEAR)]
    chip_groups = [turned(list(range(c, n, 2)), CHIP_TURN) for c in range(2)]
    var_groups = [turned(list(range(m)), VAR_TURN)]
    core_groups = [[s, s + 1] for s in range(0, n, 2)]
    f32, bf16 = jnp.float32, jnp.bfloat16
    sds = jax.ShapeDtypeStruct

    def far_groups(turn):
        return [turned(list(range(i, n, NEAR)), turn) for i in range(NEAR)]

    def exchanged(x, groups):
        return lax.all_to_all(x, "subj", 0, 0, tiled=True, axis_index_groups=groups)

    def gathered(field):
        return lax.all_gather(field, "subj", axis_index_groups=near_groups)

    def fetched(lists, near, turn):
        packed = call(
            functools.partial(pack_kernel, here, block, turn),
            sds((far, slots, width, block), bf16),
            [SMEM, VMEM],
        )(lists, near)
        return exchanged(packed, far_groups(turn))

    lists = call(
        functools.partial(list_kernel, here), sds((far, 8, LANES), jnp.int32), [SMEM], mib=62
    )(kin_index.T)
    lists = exchanged(lists, far_groups(LIST_TURN))[:, :4, :tiles]
    near = gathered(traits.T)
    local, held = call(
        functools.partial(local_kernel, here, block),
        [sds((width, rows_here), f32), sds(kin_tiles.shape, bf16)],
        [SMEM, VMEM, HBM],
        [pltpu.SemaphoreType.DMA],
    )(lists, near, kin_tiles)
    first, sent = call(
        functools.partial(first_kernel, here, block),
        [sds((width, rows_here), f32), sds((width, rows_here), bf16)],
        [SMEM, VMEM, VMEM, VMEM],
    )(lists, local, fetched(lists, near, TRAIT_TURN), held)
    copies = call(
        functools.partial(second_kernel, here, block),
        sds((m, width, rows_here), bf16),
        [SMEM, VMEM, VMEM, VMEM, VMEM, VMEM],
        [pltpu.VMEM((width, rows_here), f32)],
    )(lists, sent, fetched(lists, gathered(sent), FIRST_TURN), held, first, near)
    wide = lax.all_to_all(copies, "var", 0, 0, tiled=True, axis_index_groups=var_groups)
    wide = wide.reshape(m * width, rows_here)

    scale = 1.0 / (127.5 * float(rows_here * n) ** 0.5)
    share = dosages.shape[1] // n
    parts = sds((2, n // 2, share, m * width), f32)
    parts = call(functools.partial(score_kernel, scale, width), parts, [VMEM, VMEM])(wide, dosages)
    both = lax.all_gather(parts[1], "subj", axis_index_groups=core_groups)
    half = sds((n // 2, share * m * width // LANES, LANES), bf16)
    half = call(add_kernel, half, [VMEM, VMEM])(parts, both)
    arrived = exchanged(half, chip_groups)
    return call(sum_kernel, sds((share, m * width), f32), [VMEM])(arrived)


def solution(mesh):
    in_specs = (P("subj", "var"), P("subj", None, None), P("subj", None), P("subj", "var"))
    out_specs = P(("var", "subj"), None)
    return jax.shard_map(
        on_device, mesh=mesh, in_specs=in_specs, out_specs=out_specs, check_vma=False
    )
```
